32 devices in a mesh: ctx: 8 (over y, x, core), tp: 4 (over z).
Axes of the slice: x: 2, y: 2, z: 4, core: 2. Of those that a mesh axis runs over, the one named last changes fastest.
Arguments:
- tokens: bfloat16 [4096, 4096], P('ctx'), may hold values from -6 to 6
- query_weight: bfloat16 [4096, 512], P(None, 'tp'), may hold values from -0.09375 to 0.09375
- key_weight: bfloat16 [4096, 512], P(None, 'tp'), may hold values from -0.09375 to 0.09375
- value_weight: bfloat16 [4096, 4096], P(None, 'tp'), may hold values from -0.09375 to 0.09375
- norm_gain: bfloat16 [4096], P('tp'), may hold values from 0.5 to 1.5
- out_weight: bfloat16 [4096, 4096], P('tp'), may hold values from -0.09375 to 0.09375
Outputs:
- attended: bfloat16 [4096, 4096], P('ctx', 'tp')
The draws below stay inside these ranges and needn't reach their ends.
All inputs are finite; a program needn't handle non-finite values.
Results may differ from the reference program's by a relative error of at most 0.03.
Values may be sent and summed in bfloat16 or wider, within the bound.
No kernel may reach another device: no remote copies, remote signals or barrier semaphores. Data moves between devices by JAX's collectives and lax.ppermute only.
A program may use at most 128 MiB of HBM per device.

```python
import jax
import jax.numpy as jnp
from jax import lax

D = 4096
H = 32
F = 16
DV = 128
TOK_DEV = 512
TOKENS = 4096
N_CTX = 8
N_TP = 4


def block_scale(stream_key, shape, split, least, largest):
    factor_of = 1.0
    for position, blocks in split:
        draws = jax.random.uniform(jax.random.fold_in(jax.random.fold_in(stream_key, 6), position), (blocks,), jnp.float32, least / len(split), largest / len(split))
        factor_of = factor_of * jnp.repeat(jnp.exp(draws), shape[position] // blocks).reshape((-1,) + (1,) * (len(shape) - 1 - position))
    return factor_of


def normal_values(stream_key, extent, scale, limit, shards=(), kind=jnp.bfloat16):
    array = scale * jax.random.normal(stream_key, extent, jnp.float32)
    if shards:
        array = array * block_scale(stream_key, extent, shards, -0.22, 0.18)
    return jnp.clip(array, -limit, limit).astype(kind)


def setup_inputs(seed: int = 0) -> dict:
    splits = jax.random.split(jax.random.key(seed), 7)
    tokens = normal_values(splits[0], (TOKENS, D), 1.0, 6.0, ((0, 8),))
    query_weight = normal_values(splits[1], (D, H * F), D ** -0.5, 0.09375, ((1, 4),))
    key_weight = normal_values(splits[2], (D, H * F), D ** -0.5, 0.09375, ((1, 4),))
    value_weight = normal_values(splits[3], (D, H * DV), D ** -0.5, 0.09375, ((1, 4),))
    norm_gain = jnp.clip(1.0 + 0.1 * jax.random.normal(splits[4], (H * DV,), jnp.float32), 0.5, 1.5).astype(jnp.bfloat16)
    out_weight = normal_values(splits[5], (H * DV, D), (H * DV) ** -0.5, 0.09375, ((0, 4),))
    return dict(tokens=tokens, query_weight=query_weight, key_weight=key_weight, value_weight=value_weight, norm_gain=norm_gain, out_weight=out_weight)


half_root = 0.7071067811865476

def widen(values):
    return lax.optimization_barrier(values).astype(jnp.float32)

def project(inputs, weight, factor):
    return (jnp.dot(inputs, weight, preferred_element_type=jnp.float32) * factor).astype(jnp.bfloat16)

def pairs_of(features):
    rows, heads, width = features.shape
    wide = widen(features)
    outer = wide[:, :, :, None] * wide[:, :, None, :] * half_root
    return outer.reshape(rows, heads, width * width).astype(jnp.bfloat16)

def reference(tokens, query_weight, key_weight, value_weight, norm_gain, out_weight):
    highest = lax.Precision.HIGHEST
    factor = F ** (-0.25)
    out_wide = out_weight.astype(jnp.float32).reshape(N_TP, H // N_TP * DV, D)
    gain_heads = norm_gain.astype(jnp.float32).reshape(H, DV)
    causal_mask = jnp.tril(jnp.ones((TOK_DEV, TOK_DEV), jnp.float32)) > 0.5

    def shard_step(carried, inputs):
        x_shard, shard_index = inputs
        prev_pairs, prev_linear, prev_values, prev_pair_sums, prev_key_sums = carried
        query_rows = project(x_shard, query_weight, factor).reshape(TOK_DEV, H, F)
        key_rows = project(x_shard, key_weight, factor).reshape(TOK_DEV, H, F)
        value_rows = project(x_shard, value_weight, 1.0).reshape(TOK_DEV, H, DV)
        query_pairs = pairs_of(query_rows)
        key_pairs = pairs_of(key_rows)
        query_wide = widen(query_rows)
        key_wide = widen(key_rows)
        value_wide = widen(value_rows)
        qpair_wide = widen(query_pairs)
        kpair_wide = widen(key_pairs)
        local_pairs = jnp.einsum('thp,thd->hpd', kpair_wide, value_wide)
        local_linear = jnp.einsum('thf,thd->hfd', key_wide, value_wide)
        local_values = lax.optimization_barrier(jnp.sum(value_wide, axis=0))
        local_pair_sums = lax.optimization_barrier(jnp.sum(kpair_wide, axis=0))
        local_key_sums = lax.optimization_barrier(jnp.sum(key_wide, axis=0))
        scores = jnp.einsum('thf,shf->hts', query_wide, key_wide)
        local_weights = jnp.where(causal_mask[None], 1.0 + scores + 0.5 * scores * scores, 0.0)
        rounded_weights = widen(local_weights.astype(jnp.bfloat16))
        numerator = prev_values[None] + jnp.einsum('thf,hfd->thd', query_wide, prev_linear, precision=highest)
        numerator = numerator + jnp.einsum('thp,hpd->thd', qpair_wide, prev_pairs, precision=highest)
        numerator = numerator + jnp.einsum('hts,shd->thd', rounded_weights, value_wide)
        denominator = shard_index.astype(jnp.float32) * TOK_DEV + jnp.einsum('thf,hf->th', query_wide, prev_key_sums, precision=highest)
        denominator = denominator + jnp.einsum('thp,hp->th', qpair_wide, prev_pair_sums, precision=highest)
        denominator = denominator + jnp.transpose(lax.optimization_barrier(jnp.sum(local_weights, axis=2)))
        ratio = numerator / denominator[:, :, None]
        spread = lax.optimization_barrier(jnp.mean(ratio * ratio, axis=2, keepdims=True))
        normalized = (ratio / jnp.sqrt(spread + 1e-06) * gain_heads[None]).astype(jnp.bfloat16)
        grouped = widen(normalized).reshape(TOK_DEV, N_TP, H // N_TP * DV)
        partial_value = jnp.einsum('tgi,gid->gtd', grouped, out_wide).astype(jnp.bfloat16)
        attended = lax.optimization_barrier(jnp.sum(widen(partial_value), axis=0)).astype(jnp.bfloat16)
        new_carry = (prev_pairs + local_pairs, prev_linear + local_linear, prev_values + local_values, prev_pair_sums + local_pair_sums, prev_key_sums + local_key_sums)
        return (new_carry, attended)
    initial = (jnp.zeros((H, F * F, DV), jnp.float32), jnp.zeros((H, F, DV), jnp.float32), jnp.zeros((H, DV), jnp.float32), jnp.zeros((H, F * F), jnp.float32), jnp.zeros((H, F), jnp.float32))
    final_states, outputs = lax.scan(shard_step, initial, (tokens.reshape(N_CTX, TOK_DEV, D), jnp.arange(N_CTX, dtype=jnp.int32)))
    return outputs.reshape(N_CTX * TOK_DEV, D)
```

```python
import functools

import jax
import jax.numpy as jnp
from jax import lax
from jax.experimental import pallas as pl
from jax.experimental.pallas import tpu as pltpu
from jax.sharding import PartitionSpec as P

F = 16
DV = 128
ROLLS = F // 2
FEATURES = 2 * F + (ROLLS - 1) * F + F
HALF_ROOT = 0.7071067811865476
DEPTH_TILE = 1024
AHEAD = 2
PIECES = 1
VMEM_LIMIT = 24 * 1024 * 1024
NT = (((1,), (1,)), ((), ()))
f32 = jnp.float32
bf16 = jnp.bfloat16


def feature_blocks(x, double):
    tokens = x.shape[1]
    blocks = [x, x * x * HALF_ROOT]
    for d in range(1, ROLLS + 1):
        rolled = jnp.concatenate([x[d:], x[:d]], axis=0)
        block = x * rolled * HALF_ROOT
        if double:
            block = block * 2.0
        blocks.append(block)
    row = lax.broadcasted_iota(jnp.int32, (F // 2, tokens), 0)
    tail = jnp.where(row == 0, 1.0, 0.0).astype(f32)
    blocks[-1] = jnp.concatenate([blocks[-1][: F // 2], tail], axis=0)
    return blocks


def in_hbm(x):
    return pltpu.with_memory_space_constraint(x, pltpu.HBM)


def in_vmem(x):
    return pltpu.with_memory_space_constraint(x, pltpu.VMEM)


def call(kernel, outputs, flops, *, smem=(), vmem=(), free=(), hbm=(), loose=(), **options):
    block = pl.BlockSpec(memory_space=pltpu.VMEM)
    raw = pl.BlockSpec(memory_space=pl.ANY)
    spaces = {"vmem": pltpu.VMEM, "hbm": pltpu.HBM, "free": jax.ShapeDtypeStruct, "raw": pltpu.HBM}
    return pl.pallas_call(
        kernel,
        in_specs=[pl.BlockSpec(memory_space=pltpu.SMEM)] * len(smem)
        + [block] * (len(vmem) + len(free))
        + [raw] * (len(hbm) + len(loose)),
        out_specs=[raw if place == "raw" else block for _, _, place in outputs],
        out_shape=[spaces[place](shape, kind) for shape, kind, place in outputs],
        compiler_params=pltpu.CompilerParams(vmem_limit_bytes=VMEM_LIMIT),
        cost_estimate=pl.CostEstimate(flops=flops, bytes_accessed=flops // 256, transcendentals=0),
        **options,
    )(*[x.reshape(1) for x in smem], *[in_vmem(x) for x in vmem], *free, *[in_hbm(x) for x in hbm], *loose)


def depth_chunks(depth):
    size = min(DEPTH_TILE, depth)
    edges = [0, size // 2] + list(range(size, depth + 1, size))
    return [(start, stop - start) for start, stop in zip(edges, edges[1:])]


def project_kernel(tokens, wq, wk, wv, q_out, k_out, v_out, state, x, w_q, w_k, w_v, acc_qk, acc_v, key_features, sems):
    rows, depth = tokens.shape
    width = wq.shape[1]
    heads = width // F
    chunks = depth_chunks(depth)
    halves = (slice(0, rows // 2), slice(rows // 2, rows))

    def copies(c):
        if c >= len(chunks):
            return ()
        begin, size = chunks[c]
        part = pl.ds(begin, size)
        pairs = [(wk.at[part, :], w_k.at[part, :]), (wq.at[part, :], w_q.at[part, :])]
        for i in range(PIECES):
            some = pl.ds(i * rows // PIECES, rows // PIECES)
            pairs.append((tokens.at[some, part], x.at[some, part]))
            some = pl.ds(begin + i * size // PIECES, size // PIECES)
            pairs.append((wv.at[some, :], w_v.at[some, :]))
        return [pltpu.make_async_copy(*pair, sems.at[c, i]) for i, pair in enumerate(pairs)]

    def start(c):
        for copy in copies(c):
            copy.start()

    for c in range(AHEAD):
        start(c)
    for c, (begin, size) in enumerate(chunks):
        for copy in copies(c):
            copy.wait()
        start(c + AHEAD)
        part = slice(begin, begin + size)
        w = jnp.concatenate([w_k[part, :], w_q[part, :]], axis=1)
        for some in halves:
            qk = jnp.dot(x[some, part], w, preferred_element_type=f32)
            values = jnp.dot(x[some, part], w_v[part, :], preferred_element_type=f32)
            if c == 0:
                acc_qk[some, :] = qk
                acc_v[some, :] = values
            elif c < len(chunks) - 1:
                acc_qk[some, :] += qk
                acc_v[some, :] += values
            else:
                acc_qk[some, :] += qk
                v_out[some, :] = (acc_v[some, :] + values).astype(bf16)
    both = (acc_qk[...] * F ** (-0.25)).astype(bf16)
    keys = both[:, :width]
    k_out[...] = keys
    q_out[...] = both[:, width:]
    turned = keys.astype(f32).T
    for h in range(heads):
        for b, block in enumerate(feature_blocks(turned[h * F : (h + 1) * F], False)):
            key_features[h, b * F : (b + 1) * F, :] = block.astype(bf16)
    ones = jnp.ones((rows, DV), bf16)
    lane = lax.broadcasted_iota(jnp.int32, (FEATURES, DV), 1)
    sums = jnp.zeros((FEATURES, DV), f32)
    for h in range(heads):
        wide = jnp.concatenate([v_out[:, h * DV : (h + 1) * DV], ones], axis=1)
        total = jnp.dot(key_features[h], wide, preferred_element_type=f32)
        state[h * FEATURES : (h + 1) * FEATURES, :] = total[:, :DV].astype(bf16)
        sums = jnp.where(lane == h, total[:, DV:], sums)
    turned_sums = sums.T
    low = turned_sums[:8, :128]
    high = jnp.concatenate([turned_sums[:8, 128:], jnp.zeros((8, 256 - FEATURES), f32)], axis=1)
    state[heads * FEATURES :, :] = jnp.concatenate([low, high], axis=0).astype(bf16)


def project(tokens, wq, wk, wv):
    rows, depth = tokens.shape
    heads = wv.shape[1] // DV
    width = heads * F
    shapes = [(rows, width), (rows, width), (rows, heads * DV), (heads * FEATURES + 16, DV)]
    return call(
        project_kernel,
        [(shape, bf16, "vmem") for shape in shapes],
        2 * rows * depth * heads * (DV + 2 * F),
        hbm=[tokens, wq, wk, wv],
        scratch_shapes=[
            pltpu.VMEM((rows, depth), bf16),
            pltpu.VMEM((depth, width), bf16),
            pltpu.VMEM((depth, width), bf16),
            pltpu.VMEM((depth, heads * DV), bf16),
            pltpu.VMEM((rows, 2 * width), f32),
            pltpu.VMEM((rows, heads * DV), f32),
            pltpu.VMEM((heads, FEATURES, rows), bf16),
            pltpu.SemaphoreType.DMA((len(depth_chunks(depth)), 2 + 2 * PIECES)),
        ],
    )


def local_kernel(start, q, k, v, numerators, denominators, features):
    rows = q.shape[0]
    turned = q[...].astype(f32).T
    for i in range(features.shape[0]):
        blocks = feature_blocks(turned[(start + i) * F : (start + i + 1) * F], True)
        features[i] = jnp.concatenate(blocks, axis=0).T.astype(bf16)
    half = rows // 2
    lane = lax.broadcasted_iota(jnp.int32, q.shape, 1)
    row = lax.broadcasted_iota(jnp.int32, (half, half), 0)
    column = lax.broadcasted_iota(jnp.int32, (half, half), 1)
    queries = q[...]
    keys = k[...]
    ones = jnp.ones((rows, DV), bf16)
    wide_lane = lax.broadcasted_iota(jnp.int32, (half, DV), 1)
    sums = [jnp.zeros((half, DV), f32)] * 2
    for i in range(numerators.shape[1] // DV):
        h = start + i
        mine = jnp.where(lane // F == h, queries, jnp.zeros_like(queries))
        values = jnp.concatenate([v[:, h * DV : (h + 1) * DV], ones], axis=1)

        def weights(top, left):
            r = lax.dot_general(
                mine[top * half : (top + 1) * half],
                keys[left * half : (left + 1) * half],
                NT,
                preferred_element_type=f32,
            )
            w = 1.0 + r + r * r * 0.5
            if top == left:
                w = jnp.where(column <= row, w, 0.0)
            return w.astype(bf16)

        upper = jnp.dot(weights(0, 0), values[:half], preferred_element_type=f32)
        lower = jnp.concatenate([weights(1, 0), weights(1, 1)], axis=1)
        lower = jnp.dot(lower, values, preferred_element_type=f32)
        for j, both in enumerate((upper, lower)):
            numerators[j * half : (j + 1) * half, i * DV : (i + 1) * DV] = both[:, :DV].astype(bf16)
            sums[j] = jnp.where(wide_lane == i, both[:, DV:], sums[j])
    for j in range(2):
        denominators[j * half : (j + 1) * half] = sums[j]


def local_attention(q, k, v, start, count):
    rows = q.shape[0]
    return call(
        functools.partial(local_kernel, start),
        [
            ((rows, count * DV), bf16, "hbm"),
            ((rows, DV), f32, "hbm"),
            ((count, rows, FEATURES), bf16, "hbm"),
        ],
        count * 4 * rows * rows * 2 * DV,
        vmem=[q, k, v],
    )


def finish_kernel(begin, shards, rounds, parts, *refs):
    me, chunk, gain, *refs = refs
    received, (w, *refs) = refs[:rounds], refs[rounds:]
    sources, (normalized, out) = refs[: 3 * parts], refs[-9:-7]
    held_features, held_numerators, held_denominators, held_w, wide, products, sems = refs[-7:]
    heads, rows, _ = held_features.shape
    split = heads // parts
    width = out.shape[1]
    part = pl.ds(begin, rows)
    columns = pl.ds(pl.multiple_of(chunk[0] * width, 128), width)
    early = []

    def fetch(source, target):
        early.append(pltpu.make_async_copy(source, target, sems.at[len(early)]))

    for i in range(parts):
        numerators, denominators, features = sources[3 * i : 3 * i + 3]
        fetch(features.at[:, part, :], held_features.at[pl.ds(i * split, split)])
        fetch(numerators.at[part, :], held_numerators.at[i])
        fetch(denominators.at[part, :], held_denominators.at[i])
    late = []
    for i in range(PIECES):
        some = pl.ds(i * (w.shape[0] // PIECES), w.shape[0] // PIECES)
        late.append(pltpu.make_async_copy(w.at[some, columns], held_w.at[some, :], sems.at[3 * parts + i]))
    for copy in early + late:
        copy.start()

    sums, states = prefix_states(shards, me[0], heads, received)
    sums = jnp.concatenate([sums[:8], sums[8:, : FEATURES - 128]], axis=1)
    sums = jnp.concatenate([sums, jnp.zeros((DV - 8, FEATURES), f32)], axis=0).T
    prefixes = []
    for h in range(heads):
        wide_sums = jnp.broadcast_to(sums[:, h : h + 1], (FEATURES, DV))
        prefixes.append(jnp.concatenate([states(h), wide_sums], axis=1).astype(bf16))
    for copy in early:
        copy.wait()
    for h in range(heads):
        products[h] = jnp.dot(held_features[h], prefixes[h], preferred_element_type=f32)
    spreads = []
    for h in range(heads):
        p, i = h // split, h % split
        numerator = products[h, :, :DV] + held_numerators[p, :, i * DV : (i + 1) * DV].astype(f32)
        denominator = products[h, :, DV:] + held_denominators[p, :, i : i + 1]
        products[h, :, :DV] = numerator / denominator
    for h in range(heads):
        ratio = products[h, :, :DV]
        spreads.append(jnp.mean(ratio * ratio, axis=1, keepdims=True))
    for h in range(heads):
        columns = slice(h * DV, (h + 1) * DV)
        scaled = products[h, :, :DV] * lax.rsqrt(spreads[h] + 1e-06) * gain[columns].astype(f32).reshape(1, DV)
        wide[:, columns] = scaled.astype(bf16)
    normalized[...] = wide[...]
    for copy in late:
        copy.wait()
    out[...] = jnp.dot(wide[...], held_w[...], preferred_element_type=f32).astype(bf16)


def finish(shards, me, chunk, gain, w, local, received, begin, rows, width, after):
    heads = sum(features.shape[0] for _, _, features in local)
    parts = len(local)
    return call(
        functools.partial(finish_kernel, begin, shards, len(received), parts),
        [((rows, heads * DV), bf16, "hbm"), ((rows, width), bf16, "free")],
        2 * heads * rows * (256 * 256 + DV * width),
        smem=[me, chunk],
        free=[gain, *received],
        hbm=[w, *[array for arrays in local for array in arrays]],
        loose=after,
        scratch_shapes=[
            pltpu.VMEM((heads, rows, FEATURES), bf16),
            pltpu.VMEM((parts, rows, heads // parts * DV), bf16),
            pltpu.VMEM((parts, rows, DV), f32),
            pltpu.VMEM((w.shape[0], width), bf16),
            pltpu.VMEM((rows, heads * DV), bf16),
            pltpu.VMEM((heads, rows, 2 * DV), f32),
            pltpu.SemaphoreType.DMA((3 * parts + PIECES,)),
        ],
    )


def partials_kernel(*refs):
    w, normalized, out = refs[:PIECES], refs[PIECES:-1], refs[-1]
    begin = 0
    w = jnp.concatenate([piece[...] for piece in w], axis=0)
    for block in normalized:
        rows = block.shape[0]
        out[0, begin : begin + rows] = jnp.dot(block[...], w, preferred_element_type=f32).astype(bf16)
        begin += rows


def partials(normalized, w, count):
    depth, columns = w.shape
    tile = columns // count
    rows = sum(block.shape[0] for block in normalized)
    whole = lambda a: pl.BlockSpec(a.shape, lambda i: (0,) * a.ndim)
    piece = lambda p: pl.BlockSpec((depth // PIECES, tile), lambda i: (p, i))
    return pl.pallas_call(
        partials_kernel,
        grid=(count,),
        in_specs=[piece(p) for p in range(PIECES)] + [whole(block) for block in normalized],
        out_specs=pl.BlockSpec((1, rows, tile), lambda i: (i, 0, 0)),
        out_shape=pltpu.HBM((count, rows, tile), bf16),
        compiler_params=pltpu.CompilerParams(vmem_limit_bytes=VMEM_LIMIT),
        cost_estimate=pl.CostEstimate(
            flops=2 * rows * depth * columns, bytes_accessed=2 * depth * columns, transcendentals=0
        ),
    )(*[in_hbm(w)] * PIECES, *[in_hbm(block) for block in normalized])


def messages_kernel(begin, count, *refs):
    chunks, refs = refs[:count], refs[count:]
    up, down, sums, *refs = refs
    *outs, held, sems = refs[-count - 2 :]
    rows = up.shape[0]
    copies = []
    for i, chunk in enumerate(chunks):
        copies.append(pltpu.make_async_copy(sums.at[chunk[0], pl.ds(begin, rows), :], held.at[i], sems.at[i]))
        copies[i].start()
    for i, (received, out) in enumerate(zip((up, down, None), outs)):
        copies[i].wait()
        out[...] = held[i] if received is None else (held[i].astype(f32) + received[...].astype(f32)).astype(bf16)


def messages(sums, chunks, up, down, begin, after):
    count = len(chunks)
    return call(
        functools.partial(messages_kernel, begin, count),
        [(up.shape, bf16, "free")] * count,
        up.size * 256,
        smem=chunks,
        free=[up, down],
        hbm=[sums],
        loose=after,
        scratch_shapes=[pltpu.VMEM((count, *up.shape), bf16), pltpu.SemaphoreType.DMA((count,))],
    )


def final_kernel(begin, own, up, down, *rest):
    out, held, sems = rest[-3:]
    rows = up.shape[0]
    middle = rows // 32 * 16
    copies = []
    for i, (start, size) in enumerate(((0, middle), (middle, rows - middle))):
        part = slice(start, start + size)
        total = own[part].astype(f32) + up[part].astype(f32) + down[part].astype(f32)
        held[part] = total.astype(bf16)
        target = out.at[pl.ds(begin + start, size), :]
        copies.append(pltpu.make_async_copy(held.at[pl.ds(start, size), :], target, sems.at[i]))
        copies[-1].start()
    for copy in copies:
        copy.wait()


def final(own, up, down, begin, rows, output):
    width = up.shape[1]
    earlier = [] if output is None else [output]
    return call(
        functools.partial(final_kernel, begin),
        [((rows, width), bf16, "raw")],
        rows * width * 64,
        free=[own, up, down],
        hbm=earlier,
        input_output_aliases={3: 0} if earlier else {},
        scratch_shapes=[pltpu.VMEM(up.shape, bf16), pltpu.SemaphoreType.DMA((2,))],
    )[0]


def reduced(first, w, rows, edges):
    line = lax.axis_size("tp")
    place = lax.axis_index("tp")
    top = line - 1

    def chunk(index):
        return jnp.clip(index, 0, top).astype(jnp.int32)

    def send(block, pairs):
        return lax.ppermute(block, "tp", pairs)

    ups = [[(z, z + 1) for z in range(step + 1)] for step in range(top)]
    downs = [[(top - z, top - z - 1) for z in range(step + 1)] for step in range(top)]
    blocks = list(zip(edges, edges[1:]))
    normalized, own, up, down = [[None] * len(blocks) for _ in range(4)]
    after = []
    for b, (begin, stop) in enumerate(blocks):
        normalized[b], sums = first(begin, stop - begin, chunk(jnp.where(place < line // 2, top, 0)), after)
        up[b] = down[b] = send(sums, ups[0] + downs[0])
        after = [sums]
    sums = partials(normalized, w, line)
    after = []
    for step in range(1, top):
        chunks = [chunk(top - step + place), chunk(place - top + step)] + ([chunk(place)] if step == top - 1 else [])
        for b, (begin, _) in enumerate(blocks):
            after = messages(sums, chunks, up[b], down[b], begin, after[:2])
            up[b], down[b] = send(after[0], ups[step]), send(after[1], downs[step])
            own[b] = after[-1]
    output = None
    for b, (begin, _) in enumerate(blocks):
        output = final(own[b], up[b], down[b], begin, rows, output)
    return output


def bit_of(me, bit):
    return ((me >> bit) & 1).astype(f32)


def join_kernel(me, mine, other, out):
    size = out.shape[0] - 16

    def read(start, count):
        part = slice(start, start + count)
        return mine[part].astype(f32) + other[part].astype(f32)

    out[:size] = jnp.where((me[0] & 1) == 1, read(size, size), read(0, size)).astype(bf16)
    out[size:] = read(2 * size, 16).astype(bf16)


def cross_kernel(high_bit, me, mine, other, out):
    odd, low, high = bit_of(me[0], 0), bit_of(me[0], high_bit - 1), bit_of(me[0], high_bit)
    own = mine[...].astype(f32) * ((1.0 - odd) + odd * (1.0 - low))
    out[...] = (own + other[...].astype(f32) * ((1.0 - odd) + odd * high)).astype(bf16)


def add_kernel(me, mine, other, out):
    out[...] = (mine[...].astype(f32) + other[...].astype(f32)).astype(bf16)


def earlier_kernel(bits, me, *refs):
    *received, out = refs
    total = jnp.zeros(out.shape, f32)
    for piece, coefficient in zip(received, half_coefficients(me[0], bits)):
        total = total + piece[...].astype(f32) * coefficient
    out[...] = total.astype(bf16)


def half_coefficients(me, bits):
    if bits < 3:
        return [bit_of(me, bit) for bit in range(1, bits)]
    odd, low, high = bit_of(me, 0), bit_of(me, bits - 2), bit_of(me, bits - 1)
    return [bit_of(me, bit) for bit in range(1, bits - 2)] + [
        (1.0 - odd) * low + odd * high,
        (1.0 - odd) * high + odd * jnp.maximum(low, high),
    ]


def prefix_states(shards, me, heads, received):
    first, mine, others = received
    size = heads // 2 * FEATURES
    odd = (me & 1) == 1
    coefficient = bit_of(me, 0)
    sums = first[2 * size : 2 * size + 16].astype(f32) * coefficient + mine[size:].astype(f32)

    def states(h):
        part = slice(h * FEATURES, (h + 1) * FEATURES)
        at = slice(h * FEATURES % size, h * FEATURES % size + FEATURES)
        low, high = mine[at].astype(f32), others[at].astype(f32)
        passed = jnp.where(odd, high, low) if h < heads // 2 else jnp.where(odd, low, high)
        return first[part].astype(f32) * coefficient + passed

    return sums, states


def exchange_rounds(shards):
    bits = shards.bit_length() - 1
    if bits < 3:
        return [[bit] * shards for bit in range(1, bits)]
    rounds = [[bit] * shards for bit in range(1, bits - 2)]
    rounds.append([bits - 1 if i & 1 else bits - 2 for i in range(shards)])
    rounds.append([bits - 2 if i & 1 else bits - 1 for i in range(shards)])
    return rounds


def per_device(tokens, query_weight, key_weight, value_weight, norm_gain, out_weight):
    rows = tokens.shape[0]
    heads = norm_gain.shape[0] // DV
    shards, line = lax.axis_size("ctx"), lax.axis_size("tp")
    me = lax.axis_index("ctx")
    bits = shards.bit_length() - 1
    plan = exchange_rounds(shards)
    q, k, v, states = project(tokens, query_weight, key_weight, value_weight)

    def swap(block, across):
        return lax.ppermute(block, "ctx", [(i, i ^ (1 << across[i])) for i in range(shards)])

    def small(kernel, operands, shape):
        return call(kernel, [(shape, bf16, "vmem")], shape[0] * shape[1] * 64, smem=[me], vmem=operands)[0]

    half = heads // 2
    shape = (half * FEATURES + 16, DV)
    first = swap(states, [0] * shards)
    passed = small(join_kernel, [states, first], shape)
    local, halves = [], []
    for turn, across in enumerate(plan):
        other = swap(passed, across)
        if len(local) < 2:
            local.append(local_attention(q, k, v, len(local) * half, half))
        halves.append(other)
        if turn < len(plan) - 1:
            kernel = functools.partial(cross_kernel, bits - 1) if turn == bits - 3 else add_kernel
            passed = small(kernel, [passed, other], shape)
            q, k, v, passed, local = lax.optimization_barrier((q, k, v, passed, local))
    while len(local) < 2:
        local.append(local_attention(q, k, v, len(local) * half, half))
    halves, local = lax.optimization_barrier((halves, local))
    mine = small(functools.partial(earlier_kernel, bits), halves, shape)
    received = [first, mine, swap(mine, [0] * shards)]
    width = out_weight.shape[1] // line

    def begin_block(begin, size, chunk, after):
        return finish(shards, me, chunk, norm_gain, out_weight, local, received, begin, size, width, after)

    return reduced(begin_block, out_weight, rows, [0, rows // 2, rows])


def solution(mesh):
    in_specs = (P("ctx", None), P(None, "tp"), P(None, "tp"), P(None, "tp"), P("tp"), P("tp", None))
    out_specs = P("ctx", "tp")
    return jax.shard_map(
        per_device, mesh=mesh, in_specs=in_specs, out_specs=out_specs, check_vma=False
    )
```

```python
import functools

import jax
import jax.numpy as jnp
from jax import lax
from jax.experimental import pallas as pl
from jax.experimental.pallas import tpu as pltpu
from jax.sharding import PartitionSpec as P

F = 16
DV = 128
ROLLS = F // 2
FEATURES = 2 * F + (ROLLS - 1) * F + F
WIDE = 256
HALF_ROOT = 0.7071067811865476
DEPTH_TILE = 1024
AHEAD = 3
PIECES = 2
VMEM_LIMIT = 24 * 1024 * 1024
NT = (((1,), (1,)), ((), ()))
f32 = jnp.float32
bf16 = jnp.bfloat16


def feature_blocks(x, double):
    tokens = x.shape[1]
    blocks = [x, x * x * HALF_ROOT]
    for d in range(1, ROLLS + 1):
        rolled = jnp.concatenate([x[d:], x[:d]], axis=0)
        block = x * rolled * HALF_ROOT
        if double:
            block = block * 2.0
        blocks.append(block)
    row = lax.broadcasted_iota(jnp.int32, (F // 2, tokens), 0)
    tail = jnp.where(row == 0, 1.0, 0.0).astype(f32)
    blocks[-1] = jnp.concatenate([blocks[-1][: F // 2], tail], axis=0)
    return blocks


def in_hbm(x):
    return pltpu.with_memory_space_constraint(x, pltpu.HBM)


def in_vmem(x):
    return pltpu.with_memory_space_constraint(x, pltpu.VMEM)


def call(kernel, outputs, flops, *, smem=(), vmem=(), free=(), hbm=(), loose=(), **options):
    block = pl.BlockSpec(memory_space=pltpu.VMEM)
    raw = pl.BlockSpec(memory_space=pl.ANY)
    spaces = {"vmem": pltpu.VMEM, "hbm": pltpu.HBM, "free": jax.ShapeDtypeStruct, "raw": pltpu.HBM}
    return pl.pallas_call(
        kernel,
        in_specs=[pl.BlockSpec(memory_space=pltpu.SMEM)] * len(smem)
        + [block] * (len(vmem) + len(free))
        + [raw] * (len(hbm) + len(loose)),
        out_specs=[raw if place == "raw" else block for _, _, place in outputs],
        out_shape=[spaces[place](shape, kind) for shape, kind, place in outputs],
        compiler_params=pltpu.CompilerParams(vmem_limit_bytes=VMEM_LIMIT),
        cost_estimate=pl.CostEstimate(flops=flops, bytes_accessed=flops // 256, transcendentals=0),
        **options,
    )(*[x.reshape(1) for x in smem], *[in_vmem(x) for x in vmem], *free, *[in_hbm(x) for x in hbm], *loose)


def depth_chunks(depth):
    size = min(DEPTH_TILE, depth)
    edges = [0, size // 2] + list(range(size, depth + 1, size))
    return [(start, stop - start) for start, stop in zip(edges, edges[1:])]


def project_kernel(tokens, wq, wk, wv, q_out, k_out, v_out, state, x, w_q, w_k, w_v, acc_qk, acc_v, key_features, sems):
    rows, depth = tokens.shape
    width = wq.shape[1]
    heads = width // F
    chunks = depth_chunks(depth)
    halves = (slice(0, rows // 2), slice(rows // 2, rows))

    def copies(c):
        if c >= len(chunks):
            return ()
        begin, size = chunks[c]
        part = pl.ds(begin, size)
        pairs = [(wk.at[part, :], w_k.at[part, :]), (wq.at[part, :], w_q.at[part, :])]
        for i in range(PIECES):
            some = pl.ds(i * rows // PIECES, rows // PIECES)
            pairs.append((tokens.at[some, part], x.at[some, part]))
            some = pl.ds(begin + i * size // PIECES, size // PIECES)
            pairs.append((wv.at[some, :], w_v.at[some, :]))
        return [pltpu.make_async_copy(*pair, sems.at[c, i]) for i, pair in enumerate(pairs)]

    def start(c):
        for copy in copies(c):
            copy.start()

    for c in range(AHEAD):
        start(c)
    for c, (begin, size) in enumerate(chunks):
        for copy in copies(c):
            copy.wait()
        start(c + AHEAD)
        part = slice(begin, begin + size)
        w = jnp.concatenate([w_k[part, :], w_q[part, :]], axis=1)
        for some in halves:
            qk = jnp.dot(x[some, part], w, preferred_element_type=f32)
            values = jnp.dot(x[some, part], w_v[part, :], preferred_element_type=f32)
            if c == 0:
                acc_qk[some, :] = qk
                acc_v[some, :] = values
            elif c < len(chunks) - 1:
                acc_qk[some, :] += qk
                acc_v[some, :] += values
            else:
                acc_qk[some, :] += qk
                v_out[some, :] = (acc_v[some, :] + values).astype(bf16)
    both = (acc_qk[...] * F ** (-0.25)).astype(bf16)
    keys = both[:, :width]
    k_out[...] = keys
    q_out[...] = both[:, width:]
    turned = keys.astype(f32).T
    for h in range(heads):
        for b, block in enumerate(feature_blocks(turned[h * F : (h + 1) * F], False)):
            key_features[h, b * F : (b + 1) * F, :] = block.astype(bf16)
    ones = jnp.ones((rows, DV), bf16)
    lane = lax.broadcasted_iota(jnp.int32, (FEATURES, DV), 1)
    sums = jnp.zeros((FEATURES, DV), f32)
    for h in range(heads):
        wide = jnp.concatenate([v_out[:, h * DV : (h + 1) * DV], ones], axis=1)
        total = jnp.dot(key_features[h], wide, preferred_element_type=f32)
        state[h * FEATURES : (h + 1) * FEATURES, :] = total[:, :DV].astype(bf16)
        sums = jnp.where(lane == h, total[:, DV:], sums)
    turned_sums = sums.T
    low = turned_sums[:8, :128]
    high = jnp.concatenate([turned_sums[:8, 128:], jnp.zeros((8, 256 - FEATURES), f32)], axis=1)
    state[heads * FEATURES :, :] = jnp.concatenate([low, high], axis=0).astype(bf16)


def project(tokens, wq, wk, wv):
    rows, depth = tokens.shape
    heads = wv.shape[1] // DV
    width = heads * F
    shapes = [(rows, width), (rows, width), (rows, heads * DV), (heads * FEATURES + 16, DV)]
    return call(
        project_kernel,
        [(shape, bf16, "vmem") for shape in shapes],
        2 * rows * depth * heads * (DV + 2 * F),
        hbm=[tokens, wq, wk, wv],
        scratch_shapes=[
            pltpu.VMEM((rows, depth), bf16),
            pltpu.VMEM((depth, width), bf16),
            pltpu.VMEM((depth, width), bf16),
            pltpu.VMEM((depth, heads * DV), bf16),
            pltpu.VMEM((rows, 2 * width), f32),
            pltpu.VMEM((rows, heads * DV), f32),
            pltpu.VMEM((heads, FEATURES, rows), bf16),
            pltpu.SemaphoreType.DMA((len(depth_chunks(depth)), 2 + 2 * PIECES)),
        ],
    )


def local_kernel(start, q, k, v, numerators, features):
    rows = q.shape[0]
    half = rows // 2
    turned = q[...].astype(f32).T
    lane = lax.broadcasted_iota(jnp.int32, q.shape, 1)
    row = lax.broadcasted_iota(jnp.int32, (half, half), 0)
    column = lax.broadcasted_iota(jnp.int32, (half, half), 1)
    queries = q[...]
    keys = k[...]
    ones = jnp.ones((rows, DV), bf16)
    tail_lane = lax.broadcasted_iota(jnp.int32, (half, WIDE - DV), 1) + DV
    padding = jnp.zeros((WIDE - FEATURES, rows), f32)
    for i in range(features.shape[0]):
        h = start + i
        blocks = feature_blocks(turned[h * F : (h + 1) * F], True)
        products = jnp.concatenate(blocks + [padding], axis=0).T
        mine = jnp.where(lane // F == h, queries, jnp.zeros_like(queries))
        values = jnp.concatenate([v[:, h * DV : (h + 1) * DV], ones], axis=1)

        def weights(top, left):
            r = lax.dot_general(
                mine[top * half : (top + 1) * half],
                keys[left * half : (left + 1) * half],
                NT,
                preferred_element_type=f32,
            )
            w = 1.0 + r + r * r * 0.5
            if top == left:
                w = jnp.where(column <= row, w, 0.0)
            return w.astype(bf16)

        upper = jnp.dot(weights(0, 0), values[:half], preferred_element_type=f32)
        lower = jnp.concatenate([weights(1, 0), weights(1, 1)], axis=1)
        lower = jnp.dot(lower, values, preferred_element_type=f32)
        for j, both in enumerate((upper, lower)):
            part = slice(j * half, (j + 1) * half)
            numerators[part, i * DV : (i + 1) * DV] = both[:, :DV].astype(bf16)
            high = both[:, DV:].astype(bf16).astype(f32)
            tail = jnp.where(tail_lane == FEATURES, high, products[part, DV:])
            tail = jnp.where(tail_lane == FEATURES + 1, both[:, DV:] - high, tail)
            features[i, part, :DV] = products[part, :DV].astype(bf16)
            features[i, part, DV:] = tail.astype(bf16)


def local_attention(q, k, v, start, count):
    rows = q.shape[0]
    return call(
        functools.partial(local_kernel, start),
        [((rows, count * DV), bf16, "hbm"), ((count, rows, WIDE), bf16, "hbm")],
        count * 4 * rows * rows * 2 * DV,
        vmem=[q, k, v],
    )


def finish_kernel(begin, shards, rounds, parts, *refs):
    me, chunk, gain, *refs = refs
    received, (w, *refs) = refs[:rounds], refs[rounds:]
    sources, (normalized, out) = refs[: 2 * parts], refs[-9:-7]
    held_features, held_numerators, held_w, wide, products, squares, sems = refs[-7:]
    heads, rows, _ = held_features.shape
    split = heads // parts
    width = out.shape[1]
    part = pl.ds(begin, rows)
    columns = pl.ds(pl.multiple_of(chunk[0] * width, 128), width)
    early = []

    def fetch(source, target):
        early.append(pltpu.make_async_copy(source, target, sems.at[len(early)]))

    for i in range(parts):
        numerators, features = sources[2 * i : 2 * i + 2]
        fetch(features.at[:, part, :], held_features.at[pl.ds(i * split, split)])
        fetch(numerators.at[part, :], held_numerators.at[i])
    late = pltpu.make_async_copy(w.at[:, columns], held_w, sems.at[2 * parts])
    for copy in early + [late]:
        copy.start()

    sums, states = prefix_states(shards, me[0], heads, received)
    sums = jnp.concatenate([sums[:8], sums[8:, : FEATURES - 128]], axis=1)
    sums = jnp.concatenate([sums, jnp.zeros((DV - 8, FEATURES), f32)], axis=0).T
    row = lax.broadcasted_iota(jnp.int32, (WIDE - FEATURES, 2 * DV), 0)
    lane = lax.broadcasted_iota(jnp.int32, (WIDE - FEATURES, 2 * DV), 1)
    below = jnp.where((row < 2) & (lane >= DV), 1.0, 0.0).astype(bf16)
    prefixes = []
    for h in range(heads):
        wide_sums = jnp.broadcast_to(sums[:, h : h + 1], (FEATURES, DV))
        above = jnp.concatenate([states(h), wide_sums], axis=1).astype(bf16)
        prefixes.append(jnp.concatenate([above, below], axis=0))
    for copy in early:
        copy.wait()
    for h in range(heads):
        products[h] = jnp.dot(held_features[h], prefixes[h], preferred_element_type=f32)
    for h in range(heads):
        p, i = h // split, h % split
        numerator = products[h, :, :DV] + held_numerators[p, :, i * DV : (i + 1) * DV].astype(f32)
        ratio = numerator / products[h, :, DV:]
        products[h, :, :DV] = ratio
        squares[h * rows : (h + 1) * rows] = (ratio * ratio).astype(bf16)
    averaging = jnp.full((DV, DV), 1.0 / DV, bf16)
    spread = jnp.dot(squares[...], averaging, preferred_element_type=f32)
    for h in range(heads):
        columns = slice(h * DV, (h + 1) * DV)
        scale = lax.rsqrt(spread[h * rows : (h + 1) * rows] + 1e-06) * gain[columns].astype(f32).reshape(1, DV)
        wide[:, columns] = (products[h, :, :DV] * scale).astype(bf16)
    normalized[...] = wide[...]
    late.wait()
    out[...] = jnp.dot(wide[...], held_w[...], preferred_element_type=f32).astype(bf16)


def finish(shards, me, chunk, gain, w, local, received, begin, rows, width, after):
    heads = sum(features.shape[0] for _, features in local)
    parts = len(local)
    return call(
        functools.partial(finish_kernel, begin, shards, len(received), parts),
        [((rows, heads * DV), bf16, "hbm"), ((rows, width), bf16, "free")],
        2 * heads * rows * (256 * 256 + DV * width),
        smem=[me, chunk],
        free=[gain, *received],
        hbm=[w, *[array for arrays in local for array in arrays]],
        loose=after,
        scratch_shapes=[
            pltpu.VMEM((heads, rows, WIDE), bf16),
            pltpu.VMEM((parts, rows, heads // parts * DV), bf16),
            pltpu.VMEM((w.shape[0], width), bf16),
            pltpu.VMEM((rows, heads * DV), bf16),
            pltpu.VMEM((heads, rows, 2 * DV), f32),
            pltpu.VMEM((heads * rows, DV), bf16),
            pltpu.SemaphoreType.DMA((2 * parts + 1,)),
        ],
    )


def partials_kernel(w, *refs):
    *normalized, out = refs
    begin = 0
    for block in normalized:
        rows = block.shape[0]
        out[0, begin : begin + rows] = jnp.dot(block[...], w[...], preferred_element_type=f32).astype(bf16)
        begin += rows


def partials(normalized, w, count):
    depth, columns = w.shape
    tile = columns // count
    rows = sum(block.shape[0] for block in normalized)
    whole = lambda a: pl.BlockSpec(a.shape, lambda i: (0,) * a.ndim)
    return pl.pallas_call(
        partials_kernel,
        grid=(count,),
        in_specs=[pl.BlockSpec((depth, tile), lambda i: (0, i))] + [whole(block) for block in normalized],
        out_specs=pl.BlockSpec((1, rows, tile), lambda i: (i, 0, 0)),
        out_shape=pltpu.HBM((count, rows, tile), bf16),
        compiler_params=pltpu.CompilerParams(vmem_limit_bytes=VMEM_LIMIT),
        cost_estimate=pl.CostEstimate(
            flops=2 * rows * depth * columns, bytes_accessed=2 * depth * columns, transcendentals=0
        ),
    )(in_hbm(w), *[in_hbm(block) for block in normalized])


def messages_kernel(begin, count, *refs):
    chunks, refs = refs[:count], refs[count:]
    up, down, sums, *refs = refs
    *outs, held, sems = refs[-count - 2 :]
    rows = up.shape[0]
    copies = []
    for i, chunk in enumerate(chunks):
        copies.append(pltpu.make_async_copy(sums.at[chunk[0], pl.ds(begin, rows), :], held.at[i], sems.at[i]))
        copies[i].start()
    for i, (received, out) in enumerate(zip((up, down, None), outs)):
        copies[i].wait()
        out[...] = held[i] if received is None else (held[i].astype(f32) + received[...].astype(f32)).astype(bf16)


def messages(sums, chunks, up, down, begin, after):
    count = len(chunks)
    return call(
        functools.partial(messages_kernel, begin, count),
        [(up.shape, bf16, "free")] * count,
        up.size * 256,
        smem=chunks,
        free=[up, down],
        hbm=[sums],
        loose=after,
        scratch_shapes=[pltpu.VMEM((count, *up.shape), bf16), pltpu.SemaphoreType.DMA((count,))],
    )


def final_kernel(begin, own, up, down, *rest):
    out, held, sems = rest[-3:]
    rows = up.shape[0]
    middle = rows // 32 * 16
    copies = []
    for i, (start, size) in enumerate(((0, middle), (middle, rows - middle))):
        part = slice(start, start + size)
        total = own[part].astype(f32) + up[part].astype(f32) + down[part].astype(f32)
        held[part] = total.astype(bf16)
        target = out.at[pl.ds(begin + start, size), :]
        copies.append(pltpu.make_async_copy(held.at[pl.ds(start, size), :], target, sems.at[i]))
        copies[-1].start()
    for copy in copies:
        copy.wait()


def final(own, up, down, begin, rows, output):
    width = up.shape[1]
    earlier = [] if output is None else [output]
    return call(
        functools.partial(final_kernel, begin),
        [((rows, width), bf16, "raw")],
        rows * width * 64,
        free=[own, up, down],
        hbm=earlier,
        input_output_aliases={3: 0} if earlier else {},
        scratch_shapes=[pltpu.VMEM(up.shape, bf16), pltpu.SemaphoreType.DMA((2,))],
    )[0]


def reduced(first, w, rows, edges):
    line = lax.axis_size("tp")
    place = lax.axis_index("tp")
    top = line - 1

    def chunk(index):
        return jnp.clip(index, 0, top).astype(jnp.int32)

    def send(block, pairs):
        return lax.ppermute(block, "tp", pairs)

    ups = [[(z, z + 1) for z in range(step + 1)] for step in range(top)]
    downs = [[(top - z, top - z - 1) for z in range(step + 1)] for step in range(top)]
    blocks = list(zip(edges, edges[1:]))
    normalized, own, up, down = [[None] * len(blocks) for _ in range(4)]
    after = []
    for b, (begin, stop) in enumerate(blocks):
        normalized[b], sums = first(begin, stop - begin, chunk(jnp.where(place < line // 2, top, 0)), after)
        up[b] = down[b] = send(sums, ups[0] + downs[0])
        after = [sums]
    sums = partials(normalized, w, line)
    after = []
    for step in range(1, top):
        chunks = [chunk(top - step + place), chunk(place - top + step)] + ([chunk(place)] if step == top - 1 else [])
        for b, (begin, _) in enumerate(blocks):
            after = messages(sums, chunks, up[b], down[b], begin, after[:2])
            up[b], down[b] = send(after[0], ups[step]), send(after[1], downs[step])
            own[b] = after[-1]
    output = None
    for b, (begin, _) in enumerate(blocks):
        output = final(own[b], up[b], down[b], begin, rows, output)
    return output


def bit_of(me, bit):
    return ((me >> bit) & 1).astype(f32)


def join_kernel(me, mine, other, out):
    size = out.shape[0] - 16

    def read(start, count):
        part = slice(start, start + count)
        return mine[part].astype(f32) + other[part].astype(f32)

    out[:size] = jnp.where((me[0] & 1) == 1, read(size, size), read(0, size)).astype(bf16)
    out[size:] = read(2 * size, 16).astype(bf16)


def cross_kernel(high_bit, me, mine, other, out):
    odd, low, high = bit_of(me[0], 0), bit_of(me[0], high_bit - 1), bit_of(me[0], high_bit)
    own = mine[...].astype(f32) * ((1.0 - odd) + odd * (1.0 - low))
    out[...] = (own + other[...].astype(f32) * ((1.0 - odd) + odd * high)).astype(bf16)


def add_kernel(me, mine, other, out):
    out[...] = (mine[...].astype(f32) + other[...].astype(f32)).astype(bf16)


def earlier_kernel(bits, me, *refs):
    *received, out = refs
    total = jnp.zeros(out.shape, f32)
    for piece, coefficient in zip(received, half_coefficients(me[0], bits)):
        total = total + piece[...].astype(f32) * coefficient
    out[...] = total.astype(bf16)


def half_coefficients(me, bits):
    if bits < 3:
        return [bit_of(me, bit) for bit in range(1, bits)]
    odd, low, high = bit_of(me, 0), bit_of(me, bits - 2), bit_of(me, bits - 1)
    return [bit_of(me, bit) for bit in range(1, bits - 2)] + [
        (1.0 - odd) * low + odd * high,
        (1.0 - odd) * high + odd * jnp.maximum(low, high),
    ]


def prefix_states(shards, me, heads, received):
    first, mine, others = received
    size = heads // 2 * FEATURES
    odd = (me & 1) == 1
    coefficient = bit_of(me, 0)
    sums = first[2 * size : 2 * size + 16].astype(f32) * coefficient + mine[size:].astype(f32)

    def states(h):
        part = slice(h * FEATURES, (h + 1) * FEATURES)
        at = slice(h * FEATURES % size, h * FEATURES % size + FEATURES)
        low, high = mine[at].astype(f32), others[at].astype(f32)
        passed = jnp.where(odd, high, low) if h < heads // 2 else jnp.where(odd, low, high)
        return first[part].astype(f32) * coefficient + passed

    return sums, states


def exchange_rounds(shards):
    bits = shards.bit_length() - 1
    if bits < 3:
        return [[bit] * shards for bit in range(1, bits)]
    rounds = [[bit] * shards for bit in range(1, bits - 2)]
    rounds.append([bits - 1 if i & 1 else bits - 2 for i in range(shards)])
    rounds.append([bits - 2 if i & 1 else bits - 1 for i in range(shards)])
    return rounds


def per_device(tokens, query_weight, key_weight, value_weight, norm_gain, out_weight):
    rows = tokens.shape[0]
    heads = norm_gain.shape[0] // DV
    shards, line = lax.axis_size("ctx"), lax.axis_size("tp")
    me = lax.axis_index("ctx")
    bits = shards.bit_length() - 1
    plan = exchange_rounds(shards)
    q, k, v, states = project(tokens, query_weight, key_weight, value_weight)

    def swap(block, across):
        return lax.ppermute(block, "ctx", [(i, i ^ (1 << across[i])) for i in range(shards)])

    def small(kernel, operands, shape):
        return call(kernel, [(shape, bf16, "vmem")], shape[0] * shape[1] * 64, smem=[me], vmem=operands)[0]

    half = heads // 2
    shape = (half * FEATURES + 16, DV)
    first = swap(states, [0] * shards)
    passed = small(join_kernel, [states, first], shape)
    local, halves = [], []
    for turn, across in enumerate(plan):
        other = swap(passed, across)
        if len(local) < 2:
            local.append(local_attention(q, k, v, len(local) * half, half))
        halves.append(other)
        if turn < len(plan) - 1:
            kernel = functools.partial(cross_kernel, bits - 1) if turn == bits - 3 else add_kernel
            passed = small(kernel, [passed, other], shape)
            q, k, v, passed, local = lax.optimization_barrier((q, k, v, passed, local))
    while len(local) < 2:
        local.append(local_attention(q, k, v, len(local) * half, half))
    halves, local = lax.optimization_barrier((halves, local))
    mine = small(functools.partial(earlier_kernel, bits), halves, shape)
    received = [first, mine, swap(mine, [0] * shards)]
    width = out_weight.shape[1] // line

    def begin_block(begin, size, chunk, after):
        return finish(shards, me, chunk, norm_gain, out_weight, local, received, begin, size, width, after)

    return reduced(begin_block, out_weight, rows, [0, rows // 2, rows])


def solution(mesh):
    in_specs = (P("ctx", None), P(None, "tp"), P(None, "tp"), P(None, "tp"), P("tp"), P("tp", None))
    out_specs = P("ctx", "tp")
    return jax.shard_map(
        per_device, mesh=mesh, in_specs=in_specs, out_specs=out_specs, check_vma=False
    )
```

```python
import functools

import jax
import jax.numpy as jnp
from jax import lax
from jax.experimental import pallas as pl
from jax.experimental.pallas import tpu as pltpu
from jax.sharding import PartitionSpec as P

F = 16
DV = 128
ROLLS = F // 2
FEATURES = 2 * F + (ROLLS - 1) * F + F
WIDE = 256
HALF_ROOT = 0.7071067811865476
DEPTH_TILE = 1024
AHEAD = 3
PIECES = 2
VMEM_LIMIT = 24 * 1024 * 1024
NT = (((1,), (1,)), ((), ()))
f32 = jnp.float32
bf16 = jnp.bfloat16


def feature_blocks(x, double):
    tokens = x.shape[1]
    blocks = [x, x * x * HALF_ROOT]
    for d in range(1, ROLLS + 1):
        rolled = jnp.concatenate([x[d:], x[:d]], axis=0)
        block = x * rolled * HALF_ROOT
        if double:
            block = block * 2.0
        blocks.append(block)
    row = lax.broadcasted_iota(jnp.int32, (F // 2, tokens), 0)
    tail = jnp.where(row == 0, 1.0, 0.0).astype(f32)
    blocks[-1] = jnp.concatenate([blocks[-1][: F // 2], tail], axis=0)
    return blocks


def in_hbm(x):
    return pltpu.with_memory_space_constraint(x, pltpu.HBM)


def in_vmem(x):
    return pltpu.with_memory_space_constraint(x, pltpu.VMEM)


def call(kernel, outputs, flops, *, smem=(), vmem=(), free=(), hbm=(), loose=(), **options):
    block = pl.BlockSpec(memory_space=pltpu.VMEM)
    raw = pl.BlockSpec(memory_space=pl.ANY)
    spaces = {"vmem": pltpu.VMEM, "hbm": pltpu.HBM, "free": jax.ShapeDtypeStruct, "raw": pltpu.HBM}
    return pl.pallas_call(
        kernel,
        in_specs=[pl.BlockSpec(memory_space=pltpu.SMEM)] * len(smem)
        + [block] * (len(vmem) + len(free))
        + [raw] * (len(hbm) + len(loose)),
        out_specs=[raw if place == "raw" else block for _, _, place in outputs],
        out_shape=[spaces[place](shape, kind) for shape, kind, place in outputs],
        compiler_params=pltpu.CompilerParams(vmem_limit_bytes=VMEM_LIMIT),
        cost_estimate=pl.CostEstimate(flops=flops, bytes_accessed=flops // 256, transcendentals=0),
        **options,
    )(*[x.reshape(1) for x in smem], *[in_vmem(x) for x in vmem], *free, *[in_hbm(x) for x in hbm], *loose)


def depth_chunks(depth):
    size = min(DEPTH_TILE, depth)
    edges = [0, size // 2] + list(range(size, depth + 1, size))
    return [(start, stop - start) for start, stop in zip(edges, edges[1:])]


def project_kernel(tokens, wq, wk, wv, q_out, k_out, v_out, state, x, w_q, w_k, w_v, acc_qk, acc_v, key_features, sems):
    rows, depth = tokens.shape
    width = wq.shape[1]
    heads = width // F
    chunks = depth_chunks(depth)
    halves = (slice(0, rows // 2), slice(rows // 2, rows))

    def copies(c):
        if c >= len(chunks):
            return ()
        begin, size = chunks[c]
        part = pl.ds(begin, size)
        pairs = [(wk.at[part, :], w_k.at[part, :]), (wq.at[part, :], w_q.at[part, :])]
        for i in range(PIECES):
            some = pl.ds(i * rows // PIECES, rows // PIECES)
            pairs.append((tokens.at[some, part], x.at[some, part]))
            some = pl.ds(begin + i * size // PIECES, size // PIECES)
            pairs.append((wv.at[some, :], w_v.at[some, :]))
        return [pltpu.make_async_copy(*pair, sems.at[c, i]) for i, pair in enumerate(pairs)]

    def start(c):
        for copy in copies(c):
            copy.start()

    for c in range(AHEAD):
        start(c)
    for c, (begin, size) in enumerate(chunks):
        for copy in copies(c):
            copy.wait()
        start(c + AHEAD)
        part = slice(begin, begin + size)
        w = jnp.concatenate([w_k[part, :], w_q[part, :]], axis=1)
        for some in halves:
            qk = jnp.dot(x[some, part], w, preferred_element_type=f32)
            values = jnp.dot(x[some, part], w_v[part, :], preferred_element_type=f32)
            if c == 0:
                acc_qk[some, :] = qk
                acc_v[some, :] = values
            elif c < len(chunks) - 1:
                acc_qk[some, :] += qk
                acc_v[some, :] += values
            else:
                acc_qk[some, :] += qk
                v_out[some, :] = (acc_v[some, :] + values).astype(bf16)
    both = (acc_qk[...] * F ** (-0.25)).astype(bf16)
    keys = both[:, :width]
    k_out[...] = keys
    q_out[...] = both[:, width:]
    turned = keys.astype(f32).T
    for h in range(heads):
        for b, block in enumerate(feature_blocks(turned[h * F : (h + 1) * F], False)):
            key_features[h, b * F : (b + 1) * F, :] = block.astype(bf16)
    ones = jnp.ones((rows, DV), bf16)
    lane = lax.broadcasted_iota(jnp.int32, (FEATURES, DV), 1)
    sums = jnp.zeros((FEATURES, DV), f32)
    for h in range(heads):
        wide = jnp.concatenate([v_out[:, h * DV : (h + 1) * DV], ones], axis=1)
        total = jnp.dot(key_features[h], wide, preferred_element_type=f32)
        state[h * FEATURES : (h + 1) * FEATURES, :] = total[:, :DV].astype(bf16)
        sums = jnp.where(lane == h, total[:, DV:], sums)
    turned_sums = sums.T
    low = turned_sums[:8, :128]
    high = jnp.concatenate([turned_sums[:8, 128:], jnp.zeros((8, 256 - FEATURES), f32)], axis=1)
    state[heads * FEATURES :, :] = jnp.concatenate([low, high], axis=0).astype(bf16)


def project(tokens, wq, wk, wv):
    rows, depth = tokens.shape
    heads = wv.shape[1] // DV
    width = heads * F
    shapes = [(rows, width), (rows, width), (rows, heads * DV), (heads * FEATURES + 16, DV)]
    return call(
        project_kernel,
        [(shape, bf16, "vmem") for shape in shapes],
        2 * rows * depth * heads * (DV + 2 * F),
        hbm=[tokens, wq, wk, wv],
        scratch_shapes=[
            pltpu.VMEM((rows, depth), bf16),
            pltpu.VMEM((depth, width), bf16),
            pltpu.VMEM((depth, width), bf16),
            pltpu.VMEM((depth, heads * DV), bf16),
            pltpu.VMEM((rows, 2 * width), f32),
            pltpu.VMEM((rows, heads * DV), f32),
            pltpu.VMEM((heads, FEATURES, rows), bf16),
            pltpu.SemaphoreType.DMA((len(depth_chunks(depth)), 2 + 2 * PIECES)),
        ],
    )


def local_kernel(start, q, k, v, numerators, features):
    rows = q.shape[0]
    half = rows // 2
    turned = q[...].astype(f32).T
    lane = lax.broadcasted_iota(jnp.int32, q.shape, 1)
    row = lax.broadcasted_iota(jnp.int32, (half, half), 0)
    column = lax.broadcasted_iota(jnp.int32, (half, half), 1)
    queries = q[...]
    keys = k[...]
    ones = jnp.ones((rows, DV), bf16)
    tail_lane = lax.broadcasted_iota(jnp.int32, (half, WIDE - DV), 1) + DV
    padding = jnp.zeros((WIDE - FEATURES, rows), f32)
    for i in range(features.shape[0]):
        h = start + i
        blocks = feature_blocks(turned[h * F : (h + 1) * F], True)
        products = jnp.concatenate(blocks + [padding], axis=0).T
        mine = jnp.where(lane // F == h, queries, jnp.zeros_like(queries))
        values = jnp.concatenate([v[:, h * DV : (h + 1) * DV], ones], axis=1)

        def weights(top, left):
            r = lax.dot_general(
                mine[top * half : (top + 1) * half],
                keys[left * half : (left + 1) * half],
                NT,
                preferred_element_type=f32,
            )
            w = 1.0 + r + r * r * 0.5
            if top == left:
                w = jnp.where(column <= row, w, 0.0)
            return w.astype(bf16)

        upper = jnp.dot(weights(0, 0), values[:half], preferred_element_type=f32)
        lower = jnp.concatenate([weights(1, 0), weights(1, 1)], axis=1)
        lower = jnp.dot(lower, values, preferred_element_type=f32)
        for j, both in enumerate((upper, lower)):
            part = slice(j * half, (j + 1) * half)
            numerators[part, i * DV : (i + 1) * DV] = both[:, :DV].astype(bf16)
            high = both[:, DV:].astype(bf16).astype(f32)
            tail = jnp.where(tail_lane == FEATURES, high, products[part, DV:])
            tail = jnp.where(tail_lane == FEATURES + 1, both[:, DV:] - high, tail)
            features[i, part, :DV] = products[part, :DV].astype(bf16)
            features[i, part, DV:] = tail.astype(bf16)


def local_attention(q, k, v, start, count):
    rows = q.shape[0]
    return call(
        functools.partial(local_kernel, start),
        [((rows, count * DV), bf16, "hbm"), ((count, rows, WIDE), bf16, "hbm")],
        count * 4 * rows * rows * 2 * DV,
        vmem=[q, k, v],
    )


def finish_kernel(begin, shards, rounds, parts, *refs):
    me, chunk, gain, *refs = refs
    received, (w, *refs) = refs[:rounds], refs[rounds:]
    sources, (normalized, out) = refs[: 2 * parts], refs[-9:-7]
    held_features, held_numerators, held_w, wide, products, squares, sems = refs[-7:]
    heads, rows, _ = held_features.shape
    split = heads // parts
    width = out.shape[1]
    part = pl.ds(begin, rows)
    columns = pl.ds(pl.multiple_of(chunk[0] * width, 128), width)
    early = []

    def fetch(source, target):
        early.append(pltpu.make_async_copy(source, target, sems.at[len(early)]))

    for i in range(parts):
        numerators, features = sources[2 * i : 2 * i + 2]
        fetch(features.at[:, part, :], held_features.at[pl.ds(i * split, split)])
        fetch(numerators.at[part, :], held_numerators.at[i])
    late = pltpu.make_async_copy(w.at[:, columns], held_w, sems.at[2 * parts])
    for copy in early + [late]:
        copy.start()

    sums, states = prefix_states(shards, me[0], heads, received)
    sums = jnp.concatenate([sums[:8], sums[8:, : FEATURES - 128]], axis=1)
    sums = jnp.concatenate([sums, jnp.zeros((DV - 8, FEATURES), f32)], axis=0).T
    row = lax.broadcasted_iota(jnp.int32, (WIDE - FEATURES, 2 * DV), 0)
    lane = lax.broadcasted_iota(jnp.int32, (WIDE - FEATURES, 2 * DV), 1)
    below = jnp.where((row < 2) & (lane >= DV), 1.0, 0.0).astype(bf16)
    prefixes = []
    for h in range(heads):
        wide_sums = jnp.broadcast_to(sums[:, h : h + 1], (FEATURES, DV))
        above = jnp.concatenate([states(h), wide_sums], axis=1).astype(bf16)
        prefixes.append(jnp.concatenate([above, below], axis=0))
    for copy in early:
        copy.wait()
    for h in range(heads):
        products[h] = jnp.dot(held_features[h], prefixes[h], preferred_element_type=f32)
    for h in range(heads):
        p, i = h // split, h % split
        numerator = products[h, :, :DV] + held_numerators[p, :, i * DV : (i + 1) * DV].astype(f32)
        ratio = numerator / products[h, :, DV:]
        products[h, :, :DV] = ratio
        squares[h * rows : (h + 1) * rows] = (ratio * ratio).astype(bf16)
    averaging = jnp.full((DV, DV), 1.0 / DV, bf16)
    spread = jnp.dot(squares[...], averaging, preferred_element_type=f32)
    for h in range(heads):
        columns = slice(h * DV, (h + 1) * DV)
        scale = lax.rsqrt(spread[h * rows : (h + 1) * rows] + 1e-06) * gain[columns].astype(f32).reshape(1, DV)
        wide[:, columns] = (products[h, :, :DV] * scale).astype(bf16)
    aside = pltpu.make_async_copy(wide, normalized, sems.at[2 * parts + 1])
    aside.start()
    late.wait()
    out[...] = jnp.dot(wide[...], held_w[...], preferred_element_type=f32).astype(bf16)
    aside.wait()


def finish(shards, me, chunk, gain, w, local, received, begin, rows, width, after):
    heads = sum(features.shape[0] for _, features in local)
    parts = len(local)
    return call(
        functools.partial(finish_kernel, begin, shards, len(received), parts),
        [((rows, heads * DV), bf16, "raw"), ((rows, width), bf16, "free")],
        2 * heads * rows * (256 * 256 + DV * width),
        smem=[me, chunk],
        free=[gain, *received],
        hbm=[w, *[array for arrays in local for array in arrays]],
        loose=after,
        scratch_shapes=[
            pltpu.VMEM((heads, rows, WIDE), bf16),
            pltpu.VMEM((parts, rows, heads // parts * DV), bf16),
            pltpu.VMEM((w.shape[0], width), bf16),
            pltpu.VMEM((rows, heads * DV), bf16),
            pltpu.VMEM((heads, rows, 2 * DV), f32),
            pltpu.VMEM((heads * rows, DV), bf16),
            pltpu.SemaphoreType.DMA((2 * parts + 2,)),
        ],
    )


def partials_kernel(w, *refs):
    *normalized, out = refs
    begin = 0
    for block in normalized:
        rows = block.shape[0]
        out[0, begin : begin + rows] = jnp.dot(block[...], w[...], preferred_element_type=f32).astype(bf16)
        begin += rows


def partials(normalized, w, count):
    depth, columns = w.shape
    tile = columns // count
    rows = sum(block.shape[0] for block in normalized)
    whole = lambda a: pl.BlockSpec(a.shape, lambda i: (0,) * a.ndim)
    return pl.pallas_call(
        partials_kernel,
        grid=(count,),
        in_specs=[pl.BlockSpec((depth, tile), lambda i: (0, i))] + [whole(block) for block in normalized],
        out_specs=pl.BlockSpec((1, rows, tile), lambda i: (i, 0, 0)),
        out_shape=pltpu.HBM((count, rows, tile), bf16),
        compiler_params=pltpu.CompilerParams(vmem_limit_bytes=VMEM_LIMIT),
        cost_estimate=pl.CostEstimate(
            flops=2 * rows * depth * columns, bytes_accessed=2 * depth * columns, transcendentals=0
        ),
    )(in_hbm(w), *[in_hbm(block) for block in normalized])


def messages_kernel(begin, count, *refs):
    chunks, refs = refs[:count], refs[count:]
    up, down, sums, *refs = refs
    *outs, held, sems = refs[-count - 2 :]
    rows = up.shape[0]
    copies = []
    for i, chunk in enumerate(chunks):
        copies.append(pltpu.make_async_copy(sums.at[chunk[0], pl.ds(begin, rows), :], held.at[i], sems.at[i]))
        copies[i].start()
    for i, (received, out) in enumerate(zip((up, down, None), outs)):
        copies[i].wait()
        out[...] = held[i] if received is None else (held[i].astype(f32) + received[...].astype(f32)).astype(bf16)


def messages(sums, chunks, up, down, begin, after):
    count = len(chunks)
    return call(
        functools.partial(messages_kernel, begin, count),
        [(up.shape, bf16, "free")] * count,
        up.size * 256,
        smem=chunks,
        free=[up, down],
        hbm=[sums],
        loose=after,
        scratch_shapes=[pltpu.VMEM((count, *up.shape), bf16), pltpu.SemaphoreType.DMA((count,))],
    )


def final_kernel(begin, own, up, down, *rest):
    out, held, sems = rest[-3:]
    rows = up.shape[0]
    middle = rows // 32 * 16
    copies = []
    for i, (start, size) in enumerate(((0, middle), (middle, rows - middle))):
        part = slice(start, start + size)
        total = own[part].astype(f32) + up[part].astype(f32) + down[part].astype(f32)
        held[part] = total.astype(bf16)
        target = out.at[pl.ds(begin + start, size), :]
        copies.append(pltpu.make_async_copy(held.at[pl.ds(start, size), :], target, sems.at[i]))
        copies[-1].start()
    for copy in copies:
        copy.wait()


def final(own, up, down, begin, rows, output):
    width = up.shape[1]
    earlier = [] if output is None else [output]
    return call(
        functools.partial(final_kernel, begin),
        [((rows, width), bf16, "raw")],
        rows * width * 64,
        free=[own, up, down],
        hbm=earlier,
        input_output_aliases={3: 0} if earlier else {},
        scratch_shapes=[pltpu.VMEM(up.shape, bf16), pltpu.SemaphoreType.DMA((2,))],
    )[0]


def reduced(first, w, rows, edges):
    line = lax.axis_size("tp")
    place = lax.axis_index("tp")
    top = line - 1

    def chunk(index):
        return jnp.clip(index, 0, top).astype(jnp.int32)

    def send(block, pairs):
        return lax.ppermute(block, "tp", pairs)

    ups = [[(z, z + 1) for z in range(step + 1)] for step in range(top)]
    downs = [[(top - z, top - z - 1) for z in range(step + 1)] for step in range(top)]
    blocks = list(zip(edges, edges[1:]))
    normalized, own, up, down = [[None] * len(blocks) for _ in range(4)]
    after = []
    for b, (begin, stop) in enumerate(blocks):
        normalized[b], sums = first(begin, stop - begin, chunk(jnp.where(place < line // 2, top, 0)), after)
        up[b] = down[b] = send(sums, ups[0] + downs[0])
        after = [sums]
    sums = partials(normalized, w, line)
    after = []
    for step in range(1, top):
        chunks = [chunk(top - step + place), chunk(place - top + step)] + ([chunk(place)] if step == top - 1 else [])
        for b, (begin, _) in enumerate(blocks):
            after = messages(sums, chunks, up[b], down[b], begin, after[:2])
            up[b], down[b] = send(after[0], ups[step]), send(after[1], downs[step])
            own[b] = after[-1]
    output = None
    for b, (begin, _) in enumerate(blocks):
        output = final(own[b], up[b], down[b], begin, rows, output)
    return output


def bit_of(me, bit):
    return ((me >> bit) & 1).astype(f32)


def join_kernel(me, mine, other, out):
    size = out.shape[0] - 16

    def read(start, count):
        part = slice(start, start + count)
        return mine[part].astype(f32) + other[part].astype(f32)

    out[:size] = jnp.where((me[0] & 1) == 1, read(size, size), read(0, size)).astype(bf16)
    out[size:] = read(2 * size, 16).astype(bf16)


def cross_kernel(high_bit, me, mine, other, out):
    odd, low, high = bit_of(me[0], 0), bit_of(me[0], high_bit - 1), bit_of(me[0], high_bit)
    own = mine[...].astype(f32) * ((1.0 - odd) + odd * (1.0 - low))
    out[...] = (own + other[...].astype(f32) * ((1.0 - odd) + odd * high)).astype(bf16)


def add_kernel(me, mine, other, out):
    out[...] = (mine[...].astype(f32) + other[...].astype(f32)).astype(bf16)


def earlier_kernel(bits, me, *refs):
    *received, out = refs
    total = jnp.zeros(out.shape, f32)
    for piece, coefficient in zip(received, half_coefficients(me[0], bits)):
        total = total + piece[...].astype(f32) * coefficient
    out[...] = total.astype(bf16)


def half_coefficients(me, bits):
    if bits < 3:
        return [bit_of(me, bit) for bit in range(1, bits)]
    odd, low, high = bit_of(me, 0), bit_of(me, bits - 2), bit_of(me, bits - 1)
    return [bit_of(me, bit) for bit in range(1, bits - 2)] + [
        (1.0 - odd) * low + odd * high,
        (1.0 - odd) * high + odd * jnp.maximum(low, high),
    ]


def prefix_states(shards, me, heads, received):
    first, mine, others = received
    size = heads // 2 * FEATURES
    odd = (me & 1) == 1
    coefficient = bit_of(me, 0)
    sums = first[2 * size : 2 * size + 16].astype(f32) * coefficient + mine[size:].astype(f32)

    def states(h):
        part = slice(h * FEATURES, (h + 1) * FEATURES)
        at = slice(h * FEATURES % size, h * FEATURES % size + FEATURES)
        low, high = mine[at].astype(f32), others[at].astype(f32)
        passed = jnp.where(odd, high, low) if h < heads // 2 else jnp.where(odd, low, high)
        return first[part].astype(f32) * coefficient + passed

    return sums, states


def exchange_rounds(shards):
    bits = shards.bit_length() - 1
    if bits < 3:
        return [[bit] * shards for bit in range(1, bits)]
    rounds = [[bit] * shards for bit in range(1, bits - 2)]
    rounds.append([bits - 1 if i & 1 else bits - 2 for i in range(shards)])
    rounds.append([bits - 2 if i & 1 else bits - 1 for i in range(shards)])
    return rounds


def per_device(tokens, query_weight, key_weight, value_weight, norm_gain, out_weight):
    rows = tokens.shape[0]
    heads = norm_gain.shape[0] // DV
    shards, line = lax.axis_size("ctx"), lax.axis_size("tp")
    me = lax.axis_index("ctx")
    bits = shards.bit_length() - 1
    plan = exchange_rounds(shards)
    q, k, v, states = project(tokens, query_weight, key_weight, value_weight)

    def swap(block, across):
        return lax.ppermute(block, "ctx", [(i, i ^ (1 << across[i])) for i in range(shards)])

    def small(kernel, operands, shape):
        return call(kernel, [(shape, bf16, "vmem")], shape[0] * shape[1] * 64, smem=[me], vmem=operands)[0]

    half = heads // 2
    shape = (half * FEATURES + 16, DV)
    first = swap(states, [0] * shards)
    passed = small(join_kernel, [states, first], shape)
    local, halves = [], []
    for turn, across in enumerate(plan):
        other = swap(passed, across)
        if len(local) < 2:
            local.append(local_attention(q, k, v, len(local) * half, half))
        halves.append(other)
        if turn < len(plan) - 1:
            kernel = functools.partial(cross_kernel, bits - 1) if turn == bits - 3 else add_kernel
            passed = small(kernel, [passed, other], shape)
            q, k, v, passed, local = lax.optimization_barrier((q, k, v, passed, local))
    while len(local) < 2:
        local.append(local_attention(q, k, v, len(local) * half, half))
    halves, local = lax.optimization_barrier((halves, local))
    mine = small(functools.partial(earlier_kernel, bits), halves, shape)
    received = [first, mine, swap(mine, [0] * shards)]
    width = out_weight.shape[1] // line

    def begin_block(begin, size, chunk, after):
        return finish(shards, me, chunk, norm_gain, out_weight, local, received, begin, size, width, after)

    return reduced(begin_block, out_weight, rows, [0, rows * 17 // 512 * 16, rows])


def solution(mesh):
    in_specs = (P("ctx", None), P(None, "tp"), P(None, "tp"), P(None, "tp"), P("tp"), P("tp", None))
    out_specs = P("ctx", "tp")
    return jax.shard_map(
        per_device, mesh=mesh, in_specs=in_specs, out_specs=out_specs, check_vma=False
    )
```

```python
import functools

import jax
import jax.numpy as jnp
from jax import lax
from jax.experimental import pallas as pl
from jax.experimental.pallas import tpu as pltpu
from jax.sharding import PartitionSpec as P

F = 16
DV = 128
ROLLS = F // 2
FEATURES = 2 * F + (ROLLS - 1) * F + F
WIDE = 256
HALF_ROOT = 0.7071067811865476
DEPTH_TILE = 1024
AHEAD = 4
PIECES = 2
VMEM_LIMIT = 24 * 1024 * 1024
NT = (((1,), (1,)), ((), ()))
f32 = jnp.float32
bf16 = jnp.bfloat16


def feature_blocks(x, double):
    tokens = x.shape[1]
    blocks = [x, x * x * HALF_ROOT]
    for d in range(1, ROLLS + 1):
        rolled = jnp.concatenate([x[d:], x[:d]], axis=0)
        block = x * rolled * HALF_ROOT
        if double:
            block = block * 2.0
        blocks.append(block)
    row = lax.broadcasted_iota(jnp.int32, (F // 2, tokens), 0)
    tail = jnp.where(row == 0, 1.0, 0.0).astype(f32)
    blocks[-1] = jnp.concatenate([blocks[-1][: F // 2], tail], axis=0)
    return blocks


def in_hbm(x):
    return pltpu.with_memory_space_constraint(x, pltpu.HBM)


def in_vmem(x):
    return pltpu.with_memory_space_constraint(x, pltpu.VMEM)


def call(kernel, outputs, flops, *, smem=(), vmem=(), free=(), hbm=(), loose=(), **options):
    block = pl.BlockSpec(memory_space=pltpu.VMEM)
    raw = pl.BlockSpec(memory_space=pl.ANY)
    spaces = {"vmem": pltpu.VMEM, "hbm": pltpu.HBM, "free": jax.ShapeDtypeStruct, "raw": pltpu.HBM}
    return pl.pallas_call(
        kernel,
        in_specs=[pl.BlockSpec(memory_space=pltpu.SMEM)] * len(smem)
        + [block] * (len(vmem) + len(free))
        + [raw] * (len(hbm) + len(loose)),
        out_specs=[raw if place == "raw" else block for _, _, place in outputs],
        out_shape=[spaces[place](shape, kind) for shape, kind, place in outputs],
        compiler_params=pltpu.CompilerParams(vmem_limit_bytes=VMEM_LIMIT),
        cost_estimate=pl.CostEstimate(flops=flops, bytes_accessed=flops // 256, transcendentals=0),
        **options,
    )(*[x.reshape(1) for x in smem], *[in_vmem(x) for x in vmem], *free, *[in_hbm(x) for x in hbm], *loose)


def depth_chunks(depth):
    size = min(DEPTH_TILE, depth)
    edges = [0, size // 2] + list(range(size, depth + 1, size))
    return [(start, stop - start) for start, stop in zip(edges, edges[1:])]


def project_kernel(tokens, wq, wk, wv, q_out, k_out, v_out, state, x, w_q, w_k, w_v, acc_qk, acc_v, key_features, sems):
    rows, depth = tokens.shape
    width = wq.shape[1]
    heads = width // F
    chunks = depth_chunks(depth)
    halves = (slice(0, rows // 2), slice(rows // 2, rows))

    def copies(c):
        if c >= len(chunks):
            return ()
        begin, size = chunks[c]
        part = pl.ds(begin, size)
        pairs = [(wk.at[part, :], w_k.at[part, :]), (wq.at[part, :], w_q.at[part, :])]
        for i in range(PIECES):
            some = pl.ds(i * rows // PIECES, rows // PIECES)
            pairs.append((tokens.at[some, part], x.at[some, part]))
            some = pl.ds(begin + i * size // PIECES, size // PIECES)
            pairs.append((wv.at[some, :], w_v.at[some, :]))
        return [pltpu.make_async_copy(*pair, sems.at[c, i]) for i, pair in enumerate(pairs)]

    def start(c):
        for copy in copies(c):
            copy.start()

    for c in range(AHEAD):
        start(c)
    for c, (begin, size) in enumerate(chunks):
        for copy in copies(c):
            copy.wait()
        start(c + AHEAD)
        part = slice(begin, begin + size)
        w = jnp.concatenate([w_k[part, :], w_q[part, :]], axis=1)
        for some in halves:
            qk = jnp.dot(x[some, part], w, preferred_element_type=f32)
            values = jnp.dot(x[some, part], w_v[part, :], preferred_element_type=f32)
            if c == 0:
                acc_qk[some, :] = qk
                acc_v[some, :] = values
            elif c < len(chunks) - 1:
                acc_qk[some, :] += qk
                acc_v[some, :] += values
            else:
                acc_qk[some, :] += qk
                v_out[some, :] = (acc_v[some, :] + values).astype(bf16)
    both = (acc_qk[...] * F ** (-0.25)).astype(bf16)
    keys = both[:, :width]
    k_out[...] = keys
    q_out[...] = both[:, width:]
    turned = keys.astype(f32).T
    for h in range(heads):
        for b, block in enumerate(feature_blocks(turned[h * F : (h + 1) * F], False)):
            key_features[h, b * F : (b + 1) * F, :] = block.astype(bf16)
    ones = jnp.ones((rows, DV), bf16)
    lane = lax.broadcasted_iota(jnp.int32, (FEATURES, DV), 1)
    sums = jnp.zeros((FEATURES, DV), f32)
    for h in range(heads):
        wide = jnp.concatenate([v_out[:, h * DV : (h + 1) * DV], ones], axis=1)
        total = jnp.dot(key_features[h], wide, preferred_element_type=f32)
        state[h * FEATURES : (h + 1) * FEATURES, :] = total[:, :DV].astype(bf16)
        sums = jnp.where(lane == h, total[:, DV:], sums)
    turned_sums = sums.T
    low = turned_sums[:8, :128]
    high = jnp.concatenate([turned_sums[:8, 128:], jnp.zeros((8, 256 - FEATURES), f32)], axis=1)
    state[heads * FEATURES :, :] = jnp.concatenate([low, high], axis=0).astype(bf16)


def project(tokens, wq, wk, wv):
    rows, depth = tokens.shape
    heads = wv.shape[1] // DV
    width = heads * F
    shapes = [(rows, width), (rows, width), (rows, heads * DV), (heads * FEATURES + 16, DV)]
    return call(
        project_kernel,
        [(shape, bf16, "vmem") for shape in shapes],
        2 * rows * depth * heads * (DV + 2 * F),
        hbm=[tokens, wq, wk, wv],
        scratch_shapes=[
            pltpu.VMEM((rows, depth), bf16),
            pltpu.VMEM((depth, width), bf16),
            pltpu.VMEM((depth, width), bf16),
            pltpu.VMEM((depth, heads * DV), bf16),
            pltpu.VMEM((rows, 2 * width), f32),
            pltpu.VMEM((rows, heads * DV), f32),
            pltpu.VMEM((heads, FEATURES, rows), bf16),
            pltpu.SemaphoreType.DMA((len(depth_chunks(depth)), 2 + 2 * PIECES)),
        ],
    )


def local_kernel(start, q, k, v, numerators, features):
    rows = q.shape[0]
    half = rows // 2
    turned = q[...].astype(f32).T
    lane = lax.broadcasted_iota(jnp.int32, q.shape, 1)
    row = lax.broadcasted_iota(jnp.int32, (half, half), 0)
    column = lax.broadcasted_iota(jnp.int32, (half, half), 1)
    queries = q[...]
    keys = k[...]
    ones = jnp.ones((rows, DV), bf16)
    tail_lane = lax.broadcasted_iota(jnp.int32, (half, WIDE - DV), 1) + DV
    padding = jnp.zeros((WIDE - FEATURES, rows), f32)
    for i in range(features.shape[0]):
        h = start + i
        blocks = feature_blocks(turned[h * F : (h + 1) * F], True)
        products = jnp.concatenate(blocks + [padding], axis=0).T
        mine = jnp.where(lane // F == h, queries, jnp.zeros_like(queries))
        values = jnp.concatenate([v[:, h * DV : (h + 1) * DV], ones], axis=1)

        def weights(top, left):
            r = lax.dot_general(
                mine[top * half : (top + 1) * half],
                keys[left * half : (left + 1) * half],
                NT,
                preferred_element_type=f32,
            )
            w = 1.0 + r + r * r * 0.5
            if top == left:
                w = jnp.where(column <= row, w, 0.0)
            return w.astype(bf16)

        upper = jnp.dot(weights(0, 0), values[:half], preferred_element_type=f32)
        lower = jnp.concatenate([weights(1, 0), weights(1, 1)], axis=1)
        lower = jnp.dot(lower, values, preferred_element_type=f32)
        for j, both in enumerate((upper, lower)):
            part = slice(j * half, (j + 1) * half)
            numerators[part, i * DV : (i + 1) * DV] = both[:, :DV].astype(bf16)
            high = both[:, DV:].astype(bf16).astype(f32)
            tail = jnp.where(tail_lane == FEATURES, high, products[part, DV:])
            tail = jnp.where(tail_lane == FEATURES + 1, both[:, DV:] - high, tail)
            features[i, part, :DV] = products[part, :DV].astype(bf16)
            features[i, part, DV:] = tail.astype(bf16)


def local_attention(q, k, v, start, count):
    rows = q.shape[0]
    return call(
        functools.partial(local_kernel, start),
        [((rows, count * DV), bf16, "hbm"), ((count, rows, WIDE), bf16, "hbm")],
        count * 4 * rows * rows * 2 * DV,
        vmem=[q, k, v],
    )


def finish_kernel(begin, shards, rounds, parts, *refs):
    me, chunk, gain, *refs = refs
    received, (w, *refs) = refs[:rounds], refs[rounds:]
    sources, (normalized, out) = refs[: 2 * parts], refs[-9:-7]
    held_features, held_numerators, held_w, wide, products, squares, sems = refs[-7:]
    heads, rows, _ = held_features.shape
    split = heads // parts
    width = out.shape[1]
    part = pl.ds(begin, rows)
    columns = pl.ds(pl.multiple_of(chunk[0] * width, 128), width)
    early = []

    def fetch(source, target):
        early.append(pltpu.make_async_copy(source, target, sems.at[len(early)]))

    for i in range(parts):
        numerators, features = sources[2 * i : 2 * i + 2]
        fetch(features.at[:, part, :], held_features.at[pl.ds(i * split, split)])
        fetch(numerators.at[part, :], held_numerators.at[i])
    late = pltpu.make_async_copy(w.at[:, columns], held_w, sems.at[2 * parts])
    for copy in early + [late]:
        copy.start()

    sums, states = prefix_states(shards, me[0], heads, received)
    sums = jnp.concatenate([sums[:8], sums[8:, : FEATURES - 128]], axis=1)
    sums = jnp.concatenate([sums, jnp.zeros((DV - 8, FEATURES), f32)], axis=0).T
    row = lax.broadcasted_iota(jnp.int32, (WIDE - FEATURES, 2 * DV), 0)
    lane = lax.broadcasted_iota(jnp.int32, (WIDE - FEATURES, 2 * DV), 1)
    below = jnp.where((row < 2) & (lane >= DV), 1.0, 0.0).astype(bf16)
    prefixes = []
    for h in range(heads):
        wide_sums = jnp.broadcast_to(sums[:, h : h + 1], (FEATURES, DV))
        above = jnp.concatenate([states(h), wide_sums], axis=1).astype(bf16)
        prefixes.append(jnp.concatenate([above, below], axis=0))
    for copy in early:
        copy.wait()
    for h in range(heads):
        products[h] = jnp.dot(held_features[h], prefixes[h], preferred_element_type=f32)
    for h in range(heads):
        p, i = h // split, h % split
        numerator = products[h, :, :DV] + held_numerators[p, :, i * DV : (i + 1) * DV].astype(f32)
        ratio = numerator / products[h, :, DV:]
        products[h, :, :DV] = ratio
        squares[h * rows : (h + 1) * rows] = (ratio * ratio).astype(bf16)
    averaging = jnp.full((DV, DV), 1.0 / DV, bf16)
    spread = jnp.dot(squares[...], averaging, preferred_element_type=f32)
    for h in range(heads):
        columns = slice(h * DV, (h + 1) * DV)
        scale = lax.rsqrt(spread[h * rows : (h + 1) * rows] + 1e-06) * gain[columns].astype(f32).reshape(1, DV)
        wide[:, columns] = (products[h, :, :DV] * scale).astype(bf16)
    normalized[...] = wide[...]
    late.wait()
    out[...] = jnp.dot(wide[...], held_w[...], preferred_element_type=f32).astype(bf16)


def finish(shards, me, chunk, gain, w, local, received, begin, rows, width, after):
    heads = sum(features.shape[0] for _, features in local)
    parts = len(local)
    return call(
        functools.partial(finish_kernel, begin, shards, len(received), parts),
        [((rows, heads * DV), bf16, "hbm"), ((rows, width), bf16, "free")],
        2 * heads * rows * (256 * 256 + DV * width),
        smem=[me, chunk],
        free=[gain, *received],
        hbm=[w, *[array for arrays in local for array in arrays]],
        loose=after,
        scratch_shapes=[
            pltpu.VMEM((heads, rows, WIDE), bf16),
            pltpu.VMEM((parts, rows, heads // parts * DV), bf16),
            pltpu.VMEM((w.shape[0], width), bf16),
            pltpu.VMEM((rows, heads * DV), bf16),
            pltpu.VMEM((heads, rows, 2 * DV), f32),
            pltpu.VMEM((heads * rows, DV), bf16),
            pltpu.SemaphoreType.DMA((2 * parts + 1,)),
        ],
    )


def partials_kernel(w, *refs):
    *normalized, out = refs
    begin = 0
    for block in normalized:
        rows = block.shape[0]
        out[0, begin : begin + rows] = jnp.dot(block[...], w[...], preferred_element_type=f32).astype(bf16)
        begin += rows


def partials(normalized, w, count):
    depth, columns = w.shape
    tile = columns // count
    rows = sum(block.shape[0] for block in normalized)
    whole = lambda a: pl.BlockSpec(a.shape, lambda i: (0,) * a.ndim)
    return pl.pallas_call(
        partials_kernel,
        grid=(count,),
        in_specs=[pl.BlockSpec((depth, tile), lambda i: (0, i))] + [whole(block) for block in normalized],
        out_specs=pl.BlockSpec((1, rows, tile), lambda i: (i, 0, 0)),
        out_shape=pltpu.HBM((count, rows, tile), bf16),
        compiler_params=pltpu.CompilerParams(vmem_limit_bytes=VMEM_LIMIT),
        cost_estimate=pl.CostEstimate(
            flops=2 * rows * depth * columns, bytes_accessed=2 * depth * columns, transcendentals=0
        ),
    )(in_hbm(w), *[in_hbm(block) for block in normalized])


def messages_kernel(begin, count, *refs):
    chunks, refs = refs[:count], refs[count:]
    up, down, sums, *refs = refs
    *outs, held, sems = refs[-count - 2 :]
    rows = up.shape[0]
    copies = []
    for i, chunk in enumerate(chunks):
        copies.append(pltpu.make_async_copy(sums.at[chunk[0], pl.ds(begin, rows), :], held.at[i], sems.at[i]))
        copies[i].start()
    for i, (received, out) in enumerate(zip((up, down, None), outs)):
        copies[i].wait()
        out[...] = held[i] if received is None else (held[i].astype(f32) + received[...].astype(f32)).astype(bf16)


def messages(sums, chunks, up, down, begin, after):
    count = len(chunks)
    return call(
        functools.partial(messages_kernel, begin, count),
        [(up.shape, bf16, "free")] * count,
        up.size * 256,
        smem=chunks,
        free=[up, down],
        hbm=[sums],
        loose=after,
        scratch_shapes=[pltpu.VMEM((count, *up.shape), bf16), pltpu.SemaphoreType.DMA((count,))],
    )


def final_kernel(begin, own, up, down, *rest):
    out, held, sems = rest[-3:]
    rows = up.shape[0]
    middle = rows // 32 * 16
    copies = []
    for i, (start, size) in enumerate(((0, middle), (middle, rows - middle))):
        part = slice(start, start + size)
        total = own[part].astype(f32) + up[part].astype(f32) + down[part].astype(f32)
        held[part] = total.astype(bf16)
        target = out.at[pl.ds(begin + start, size), :]
        copies.append(pltpu.make_async_copy(held.at[pl.ds(start, size), :], target, sems.at[i]))
        copies[-1].start()
    for copy in copies:
        copy.wait()


def final(own, up, down, begin, rows, output):
    width = up.shape[1]
    earlier = [] if output is None else [output]
    return call(
        functools.partial(final_kernel, begin),
        [((rows, width), bf16, "raw")],
        rows * width * 64,
        free=[own, up, down],
        hbm=earlier,
        input_output_aliases={3: 0} if earlier else {},
        scratch_shapes=[pltpu.VMEM(up.shape, bf16), pltpu.SemaphoreType.DMA((2,))],
    )[0]


def reduced(first, w, rows, edges):
    line = lax.axis_size("tp")
    place = lax.axis_index("tp")
    top = line - 1

    def chunk(index):
        return jnp.clip(index, 0, top).astype(jnp.int32)

    def send(block, pairs):
        return lax.ppermute(block, "tp", pairs)

    ups = [[(z, z + 1) for z in range(step + 1)] for step in range(top)]
    downs = [[(top - z, top - z - 1) for z in range(step + 1)] for step in range(top)]
    blocks = list(zip(edges, edges[1:]))
    normalized, own, up, down = [[None] * len(blocks) for _ in range(4)]
    after = []
    for b, (begin, stop) in enumerate(blocks):
        normalized[b], sums = first(begin, stop - begin, chunk(jnp.where(place < line // 2, top, 0)), after)
        up[b] = down[b] = send(sums, ups[0] + downs[0])
        after = [sums]
    sums = partials(normalized, w, line)
    after = []
    for step in range(1, top):
        chunks = [chunk(top - step + place), chunk(place - top + step)] + ([chunk(place)] if step == top - 1 else [])
        for b, (begin, _) in enumerate(blocks):
            after = messages(sums, chunks, up[b], down[b], begin, after[:2])
            up[b], down[b] = send(after[0], ups[step]), send(after[1], downs[step])
            own[b] = after[-1]
    output = None
    for b, (begin, _) in enumerate(blocks):
        output = final(own[b], up[b], down[b], begin, rows, output)
    return output


def bit_of(me, bit):
    return ((me >> bit) & 1).astype(f32)


def join_kernel(me, mine, other, out):
    size = out.shape[0] - 16

    def read(start, count):
        part = slice(start, start + count)
        return mine[part].astype(f32) + other[part].astype(f32)

    out[:size] = jnp.where((me[0] & 1) == 1, read(size, size), read(0, size)).astype(bf16)
    out[size:] = read(2 * size, 16).astype(bf16)


def cross_kernel(high_bit, me, mine, other, out):
    odd, low, high = bit_of(me[0], 0), bit_of(me[0], high_bit - 1), bit_of(me[0], high_bit)
    own = mine[...].astype(f32) * ((1.0 - odd) + odd * (1.0 - low))
    out[...] = (own + other[...].astype(f32) * ((1.0 - odd) + odd * high)).astype(bf16)


def add_kernel(me, mine, other, out):
    out[...] = (mine[...].astype(f32) + other[...].astype(f32)).astype(bf16)


def earlier_kernel(bits, me, *refs):
    *received, out = refs
    total = jnp.zeros(out.shape, f32)
    for piece, coefficient in zip(received, half_coefficients(me[0], bits)):
        total = total + piece[...].astype(f32) * coefficient
    out[...] = total.astype(bf16)


def half_coefficients(me, bits):
    if bits < 3:
        return [bit_of(me, bit) for bit in range(1, bits)]
    odd, low, high = bit_of(me, 0), bit_of(me, bits - 2), bit_of(me, bits - 1)
    return [bit_of(me, bit) for bit in range(1, bits - 2)] + [
        (1.0 - odd) * low + odd * high,
        (1.0 - odd) * high + odd * jnp.maximum(low, high),
    ]


def prefix_states(shards, me, heads, received):
    first, mine, others = received
    size = heads // 2 * FEATURES
    odd = (me & 1) == 1
    coefficient = bit_of(me, 0)
    sums = first[2 * size : 2 * size + 16].astype(f32) * coefficient + mine[size:].astype(f32)

    def states(h):
        part = slice(h * FEATURES, (h + 1) * FEATURES)
        at = slice(h * FEATURES % size, h * FEATURES % size + FEATURES)
        low, high = mine[at].astype(f32), others[at].astype(f32)
        passed = jnp.where(odd, high, low) if h < heads // 2 else jnp.where(odd, low, high)
        return first[part].astype(f32) * coefficient + passed

    return sums, states


def exchange_rounds(shards):
    bits = shards.bit_length() - 1
    if bits < 3:
        return [[bit] * shards for bit in range(1, bits)]
    rounds = [[bit] * shards for bit in range(1, bits - 2)]
    rounds.append([bits - 1 if i & 1 else bits - 2 for i in range(shards)])
    rounds.append([bits - 2 if i & 1 else bits - 1 for i in range(shards)])
    return rounds


def per_device(tokens, query_weight, key_weight, value_weight, norm_gain, out_weight):
    rows = tokens.shape[0]
    heads = norm_gain.shape[0] // DV
    shards, line = lax.axis_size("ctx"), lax.axis_size("tp")
    me = lax.axis_index("ctx")
    bits = shards.bit_length() - 1
    plan = exchange_rounds(shards)
    q, k, v, states = project(tokens, query_weight, key_weight, value_weight)

    def swap(block, across):
        return lax.ppermute(block, "ctx", [(i, i ^ (1 << across[i])) for i in range(shards)])

    def small(kernel, operands, shape):
        return call(kernel, [(shape, bf16, "vmem")], shape[0] * shape[1] * 64, smem=[me], vmem=operands)[0]

    half = heads // 2
    shape = (half * FEATURES + 16, DV)
    first = swap(states, [0] * shards)
    passed = small(join_kernel, [states, first], shape)
    local, halves = [], []
    for turn, across in enumerate(plan):
        other = swap(passed, across)
        if len(local) < 2:
            local.append(local_attention(q, k, v, len(local) * half, half))
        halves.append(other)
        if turn < len(plan) - 1:
            kernel = functools.partial(cross_kernel, bits - 1) if turn == bits - 3 else add_kernel
            passed = small(kernel, [passed, other], shape)
            q, k, v, passed, local = lax.optimization_barrier((q, k, v, passed, local))
    while len(local) < 2:
        local.append(local_attention(q, k, v, len(local) * half, half))
    halves, local = lax.optimization_barrier((halves, local))
    mine = small(functools.partial(earlier_kernel, bits), halves, shape)
    received = [first, mine, swap(mine, [0] * shards)]
    width = out_weight.shape[1] // line

    def begin_block(begin, size, chunk, after):
        return finish(shards, me, chunk, norm_gain, out_weight, local, received, begin, size, width, after)

    return reduced(begin_block, out_weight, rows, [0, rows // 2, rows])


def solution(mesh):
    in_specs = (P("ctx", None), P(None, "tp"), P(None, "tp"), P(None, "tp"), P("tp"), P("tp", None))
    out_specs = P("ctx", "tp")
    return jax.shard_map(
        per_device, mesh=mesh, in_specs=in_specs, out_specs=out_specs, check_vma=False
    )
```
